512 devices in a mesh: rep: 8 (over y_lo, core), fsdp: 64 (over y_hi, z, x).
Axes of the slice: x: 4, y: 8 (y_hi: 2, y_lo: 4; y = y_hi * 4 + y_lo), z: 8, core: 2. Of those that a mesh axis runs over, the one named last changes fastest.
Arguments:
- grad_parts: bfloat16 [8, 64, 128, 6144], P('rep', 'fsdp'), may hold values from -6 to 6
- master: float32 [8, 128, 6144], P('rep', None, 'fsdp'), may hold values from -6 to 6
- moment1: float32 [8, 128, 6144], P('rep', None, 'fsdp'), may hold values from -6 to 6
- moment2: float32 [8, 128, 6144], P('rep', None, 'fsdp'), may hold values from 0.1 to 4
- probe: float32 [6144], P('fsdp'), may hold values from -0.078125 to 0.078125
- flagged: int32 [8], replicated, may hold values from 0 to 511, as said below
- source: int32 [8], replicated, may hold values from 0 to 7, as said below
- step_count: int32 [1], replicated, may hold values from 1 to 11
Outputs:
- new_master: float32 [8, 128, 6144], P('rep', None, 'fsdp')
- new_moment1: float32 [8, 128, 6144], P('rep', None, 'fsdp')
- new_moment2: float32 [8, 128, 6144], P('rep', None, 'fsdp')
- params: bfloat16 [8, 128, 6144], P('rep', None, 'fsdp')
- checksum: float32 [8, 128], P('rep')
The draws below stay inside these ranges and needn't reach their ends.
Inputs may be any that keep to these rules, and one draw needn't show every extreme that they name: `flagged`: 8 devices, no two with the same shard. source[k] differs from flagged[k] // 64.
All inputs are finite; a program needn't handle non-finite values.
Results may differ from the reference program's by a relative error of at most 0.001.
Values sent between devices are 32-bit elements; how exact they have to be, the bound alone decides.
No kernel may reach another device: no remote copies, remote signals or barrier semaphores. Data moves between devices by JAX's collectives and lax.ppermute only.
A program may use at most 64 MiB of HBM per device.

```python
import math
import jax
import jax.numpy as jnp
from jax import lax

FEAT = 128
NFLAG = 8
QKV = 6144
REPLICAS = 8
SHARDS = 64


def failure_plan(key):
    shard_keys = jax.random.fold_in(key, 11)
    replica_keys = jax.random.fold_in(key, 12)
    offset_keys = jax.random.fold_in(key, 13)
    shard_pick = jax.random.permutation(shard_keys, SHARDS)[:NFLAG].astype(jnp.int32)
    replica_pick = jax.random.randint(replica_keys, (NFLAG,), 0, REPLICAS).astype(jnp.int32)
    offsets = jax.random.randint(offset_keys, (NFLAG,), 1, REPLICAS).astype(jnp.int32)
    return (shard_pick, replica_pick, offsets)


def draw_flagged(key, part):
    shard_pick, replica_pick, offsets = failure_plan(key)
    return (replica_pick * SHARDS + shard_pick).astype(jnp.int32)


def draw_source(key, part):
    shard_pick, replica_pick, offsets = failure_plan(key)
    return ((replica_pick + offsets) % REPLICAS).astype(jnp.int32)


def strengthened(drawn, key, source, target, blocks, factor):
    def block_of(position):
        return (jnp.arange(drawn.shape[position]) // (drawn.shape[position] // blocks)).reshape((-1,) + (1,) * (drawn.ndim - 1 - position))

    near = jax.random.permutation(key, blocks)[block_of(target)]
    second = (block_of(target) + blocks // 2) % blocks
    return jnp.where((block_of(source) == near) | (block_of(source) == second), factor * drawn, drawn)


def shard_levels(own_key, dims, cuts, smallest, high):
    level, own = 1.0, jax.random.fold_in(own_key, 6)
    for dim, shards_of in cuts:
        heights = jnp.exp(jax.random.uniform(jax.random.fold_in(own, dim), (shards_of,), jnp.float32, smallest / len(cuts), high / len(cuts)))
        level = level * jnp.repeat(heights, dims[dim] // shards_of).reshape([-1 if axis == dim else 1 for axis in range(len(dims))])
    return level


def centred(rng, extent, deviation, bound, split=(), dtype=jnp.bfloat16):
    drawn = jax.random.normal(rng, extent, jnp.float32) * deviation
    if len(split) > 0:
        drawn = shard_levels(rng, extent, split, -0.22, 0.18) * drawn
    return jnp.clip(drawn, min=-bound, max=bound).astype(dtype)


def bell_draw_with(key, shape, scale, reach, split, heavy, dtype=jnp.bfloat16):
    array = scale * jax.random.normal(key, shape, jnp.float32)
    if split:
        array = array * shard_levels(key, shape, split, -0.22, 0.18)
    return jnp.clip(strengthened(array, jax.random.fold_in(key, 3), *heavy), -reach, reach).astype(dtype)


def setup_inputs(seed: int = 0) -> dict:
    seeds = jax.random.split(jax.random.key(seed), 9)
    grad_parts = bell_draw_with(seeds[0], (REPLICAS, SHARDS, FEAT, QKV), 0.25, 6.0, ((0, 8), (1, 64)), (1, 3, 64, 4.0))
    master = centred(seeds[1], (REPLICAS, FEAT, QKV), 1.0, 6.0, ((0, 8), (2, 64)), jnp.float32)
    moment1 = centred(seeds[2], (REPLICAS, FEAT, QKV), 0.5, 6.0, ((0, 8), (2, 64)), jnp.float32)
    moment2 = jnp.clip(jnp.exp(math.log(4.0) - 3.6888794 * jax.random.uniform(seeds[3], (REPLICAS, FEAT, QKV), jnp.float32) ** shard_levels(seeds[3], (REPLICAS, FEAT, QKV), ((0, 8), (2, 64)), -0.2, 0.2)), 0.1, 4.0)
    probe = centred(seeds[4], (QKV,), QKV ** -0.5, 0.078125, ((0, 64),), jnp.float32)
    flagged = draw_flagged(jax.random.fold_in(seeds[8], 71), 0)
    source = draw_source(jax.random.fold_in(seeds[8], 71), 0)
    step_count = jax.random.randint(seeds[7], (1,), 1, 12).astype(jnp.int32)
    return {"grad_parts": grad_parts, "master": master, "moment1": moment1, "moment2": moment2, "probe": probe, "flagged": flagged, "source": source, "step_count": step_count}


beta_one = 0.9
beta_two = 0.95
learn_rate = 0.05
decay_rate = 0.1
epsilon = 1e-08

def reference(grad_parts, master, moment1, moment2, probe, flagged, source, step_count):
    flat_parts = grad_parts.reshape(REPLICAS * SHARDS, FEAT, QKV)

    def add_part(total, piece):
        return (total + piece.astype(jnp.float32), None)
    grad, _ = lax.scan(add_part, jnp.zeros((FEAT, QKV), jnp.float32), flat_parts)
    device_ids = jnp.arange(REPLICAS * SHARDS).astype(jnp.int32)
    hits = device_ids[:, None] == flagged[None, :]
    own_replica = (device_ids // SHARDS).astype(jnp.int32)
    donor_table = jnp.where(jnp.any(hits, axis=1), lax.optimization_barrier(jnp.sum(jnp.where(hits, source[None, :], 0), axis=1)), own_replica)
    donor_table = donor_table.astype(jnp.int32).reshape(REPLICAS, SHARDS)
    width = QKV // SHARDS

    def heal(values):
        blocks = values.reshape(REPLICAS, FEAT, SHARDS, width)
        index = jnp.broadcast_to(donor_table[:, None, :, None], blocks.shape)
        return jnp.take_along_axis(blocks, index, axis=0).reshape(REPLICAS, FEAT, QKV)
    healed_master = heal(master)
    healed_first = heal(moment1)
    healed_second = heal(moment2)
    new_first = beta_one * healed_first + (1.0 - beta_one) * grad[None]
    new_second = beta_two * healed_second + (1.0 - beta_two) * (grad * grad)[None]
    steps_done = step_count[0].astype(jnp.float32)
    correct_one = 1.0 - jnp.power(jnp.float32(beta_one), steps_done)
    correct_two = 1.0 - jnp.power(jnp.float32(beta_two), steps_done)
    update = new_first / correct_one / (jnp.sqrt(new_second / correct_two) + epsilon)
    new_master = healed_master - learn_rate * (update + decay_rate * healed_master)
    params = new_master.astype(jnp.bfloat16)
    checksum = lax.optimization_barrier(jnp.sum(new_master * probe[None, None, :], axis=2))
    return (new_master, new_first, new_second, params, checksum)
```

```python
import jax
import jax.numpy as jnp
from jax import lax
from jax.sharding import Mesh, PartitionSpec as P

beta_one = 0.9
beta_two = 0.95
learn_rate = 0.05
decay_rate = 0.1
epsilon = 1e-08

YL, C, YH, Z, X = 4, 2, 2, 8, 4
REP = ("yl", "c")
FSDP = ("yh", "z", "x")
WIDTH, HALF, FEAT = 96, 48, 128


def swapped(value, axis, size, bit):
    return lax.ppermute(value, axis, [(i, i ^ bit) for i in range(size)])


def adamw_update(master, first, second, grad, step_count):
    new_first = beta_one * first + (1.0 - beta_one) * grad
    new_second = beta_two * second + (1.0 - beta_two) * (grad * grad)
    steps_done = step_count[0].astype(jnp.float32)
    correct_one = 1.0 - jnp.power(jnp.float32(beta_one), steps_done)
    correct_two = 1.0 - jnp.power(jnp.float32(beta_two), steps_done)
    update = new_first / correct_one / (jnp.sqrt(new_second / correct_two) + epsilon)
    new_master = master - learn_rate * (update + decay_rate * master)
    return (new_master, new_first, new_second)


def reduced_grad(grad_parts):
    core = lax.axis_index("c")
    columns = grad_parts[0, 0].T.astype(jnp.float32)
    columns = columns.reshape(YH, Z, X, C, HALF, FEAT).transpose(3, 1, 2, 0, 4, 5)
    kept = jnp.where(core == 0, columns[0], columns[1])
    given = jnp.where(core == 0, columns[1], columns[0])
    chip = kept + swapped(given, "c", C, 1)
    blocks = lax.all_to_all(chip.reshape(Z * X, YH * HALF, FEAT), ("z", "x"), 0, 0, tiled=True)
    plane = jnp.sum(blocks, axis=0).reshape(YH, 1, HALF, FEAT)
    spread = jnp.broadcast_to(plane, (YH, YL, HALF, FEAT)).reshape(YH * YL, HALF, FEAT)
    lines = lax.all_to_all(spread, ("yh", "yl"), 0, 0, tiled=True)
    half = jnp.sum(lines, axis=0)
    return lax.all_gather(half, "c", axis=0, tiled=True)


def healed_state(state, flagged, source):
    my_replica = lax.axis_index(REP)
    my_shard = lax.axis_index(FSDP)
    match = flagged % (YH * Z * X) == my_shard
    replica = flagged // (YH * Z * X)
    step = jnp.sum(jnp.where(match, replica ^ source, 0))
    flagged_here = jnp.any(match & (replica == my_replica))
    moved = state
    for axis, size, bit, place in (("c", C, 1, 1), ("yl", YL, 1, 2), ("yl", YL, 2, 4)):
        other = swapped(moved, axis, size, bit)
        moved = jnp.where((step & place) != 0, other, moved)
    return jnp.where(flagged_here, moved, state)


def shards(grad_parts, master, moment1, moment2, probe, flagged, source, step_count):
    grad = reduced_grad(grad_parts)
    state = jnp.stack([master[0].T, moment1[0].T, moment2[0].T])
    healed = healed_state(state, flagged, source)
    new_master, new_first, new_second = adamw_update(
        healed[0], healed[1], healed[2], grad, step_count
    )
    local_sums = jnp.sum(new_master * probe[:, None], axis=0)
    spread = jnp.broadcast_to(local_sums, (Z * X, FEAT))
    plane_sums = jnp.sum(lax.all_to_all(spread, ("z", "x"), 0, 0, tiled=True), axis=0)
    checksum = plane_sums + swapped(plane_sums, "yh", YH, 1)
    params = new_master.astype(jnp.bfloat16)
    return (
        new_master.T[None],
        new_first.T[None],
        new_second.T[None],
        params.T[None],
        checksum.reshape(1, -1),
    )


def solution(mesh):
    named = Mesh(mesh.devices.reshape(YL, C, YH, Z, X), REP + FSDP)
    state = P(REP, None, FSDP)
    placed = (P(REP, FSDP, None, None), state, state, state, P(FSDP), P(), P(), P())
    return jax.shard_map(
        shards,
        mesh=named,
        in_specs=placed,
        out_specs=(state, state, state, state, P(REP, None)),
        check_vma=False,
    )
```

```python
import jax
import jax.numpy as jnp
from jax import lax
from jax.experimental import pallas as pl
from jax.experimental.pallas import tpu as pltpu
from jax.sharding import Mesh, PartitionSpec as P

beta_one = 0.9
beta_two = 0.95
learn_rate = 0.05
decay_rate = 0.1
epsilon = 1e-08

YL, C, YH, Z, X = 4, 2, 2, 8, 4
REP = ("yl", "c")
FSDP = ("yh", "z", "x")
WIDTH, HALF, FEAT = 96, 64, 128
TURN_STEPS = 8


def swapped(value, axis, size, bit):
    return lax.ppermute(value, axis, [(i, i ^ bit) for i in range(size)])


def adamw_update(master, first, second, grad, step_count):
    new_first = beta_one * first + (1.0 - beta_one) * grad
    new_second = beta_two * second + (1.0 - beta_two) * (grad * grad)
    steps_done = step_count[0].astype(jnp.float32)
    correct_one = 1.0 - jnp.power(jnp.float32(beta_one), steps_done)
    correct_two = 1.0 - jnp.power(jnp.float32(beta_two), steps_done)
    update = new_first / correct_one / (jnp.sqrt(new_second / correct_two) + epsilon)
    new_master = master - learn_rate * (update + decay_rate * master)
    return (new_master, new_first, new_second)


def turn_kernel(half_ref, grad_ref, turned_ref):
    columns = Z * X * WIDTH
    wide = columns // TURN_STEPS
    for i in range(TURN_STEPS):
        first = grad_ref[:, i * wide : (i + 1) * wide]
        second = grad_ref[:, columns + i * wide : columns + (i + 1) * wide]
        both = jnp.concatenate([first, second], axis=0)
        turned_ref[i * wide : (i + 1) * wide, :] = both.T.astype(jnp.float32)


def turned(grad, half):
    columns = Z * X * WIDTH
    return pl.pallas_call(
        turn_kernel,
        grid_spec=pltpu.PrefetchScalarGridSpec(
            num_scalar_prefetch=1,
            grid=(1,),
            in_specs=[pl.BlockSpec((HALF, YH * columns), lambda i, half_ref: (half_ref[0], 0))],
            out_specs=pl.BlockSpec(memory_space=pltpu.VMEM),
        ),
        out_shape=pltpu.VMEM((columns, FEAT), jnp.float32),
        cost_estimate=pl.CostEstimate(flops=0, bytes_accessed=columns * FEAT * 6, transcendentals=0),
    )(half.reshape(1), grad)


def chip_sum(grad_parts, beside):
    core = lax.axis_index("c")
    grad = grad_parts[0, 0]
    given = swapped(turned(grad, 1 - core), "c", C, 1)
    kept, beside = lax.optimization_barrier((turned(grad, core), beside))
    return kept + given, beside


def reduced_grad(chip, beside):
    blocks = lax.all_to_all(chip.reshape(Z * X, WIDTH, FEAT), ("z", "x"), 0, 0, tiled=True)
    plane = jnp.sum(blocks, axis=0)
    plane, beside = lax.optimization_barrier((plane, beside))
    spread = jnp.broadcast_to(plane, (YH * YL, WIDTH, FEAT))
    lines = lax.all_to_all(spread, ("yh", "yl"), 0, 0, tiled=True)
    line = jnp.sum(lines, axis=0)
    return lax.all_gather(line, "c", axis=0, tiled=False), beside


def healed_state(state, flagged, source):
    my_replica = lax.axis_index(REP)
    my_shard = lax.axis_index(FSDP)
    match = flagged % (YH * Z * X) == my_shard
    replica = flagged // (YH * Z * X)
    step = jnp.sum(jnp.where(match, replica ^ source, 0))
    flagged_here = jnp.any(match & (replica == my_replica))
    moved = state
    for axis, size, bit, place in (("c", C, 1, 1), ("yl", YL, 1, 2), ("yl", YL, 2, 4)):
        other = swapped(moved, axis, size, bit)
        moved = jnp.where((step & place) != 0, other, moved)
    return jnp.where(flagged_here, moved, state)


def shards(grad_parts, master, moment1, moment2, probe, flagged, source, step_count):
    my_half = lax.axis_index("yh")
    chip, state = chip_sum(grad_parts, (master[0].T, moment1[0].T, moment2[0].T))
    state = jnp.stack(state).reshape(3 * WIDTH, FEAT)
    healed = healed_state(state, flagged, source)
    weights = jnp.pad(jnp.broadcast_to(probe, (8, WIDTH)), ((0, 0), (0, FEAT - WIDTH)))
    mine = jnp.concatenate([healed, weights])
    other = swapped(mine, "yh", YH, 1)
    low, high = jnp.where(my_half == 0, mine, other), jnp.where(my_half == 0, other, mine)
    packed = jnp.stack(
        [
            jnp.concatenate([low[: 3 * WIDTH, :HALF], high[: 3 * WIDTH, :HALF]], axis=1),
            jnp.concatenate([low[: 3 * WIDTH, HALF:], high[: 3 * WIDTH, HALF:]], axis=1),
        ]
    )
    first_lanes = lax.broadcasted_iota(jnp.int32, (WIDTH, FEAT), 1) < HALF
    weights = jnp.where(
        first_lanes, low[3 * WIDTH, :WIDTH, None], high[3 * WIDTH, :WIDTH, None]
    )
    grad, (packed, weights) = reduced_grad(chip, (packed, weights))
    states = packed.reshape(C, 3, WIDTH, FEAT)
    news = adamw_update(states[:, 0], states[:, 1], states[:, 2], grad, step_count)
    lane_sums = jnp.sum(news[0] * weights, axis=1)
    local_sums = (lane_sums[:, :HALF] + lane_sums[:, HALF:]).reshape(FEAT)
    spread = jnp.broadcast_to(local_sums, (Z * X, FEAT))
    checksum = jnp.sum(lax.all_to_all(spread, ("z", "x"), 0, 0, tiled=True), axis=0)

    def own(value):
        mine = jnp.where(my_half == 0, value[:, :, :HALF], value[:, :, HALF:])
        return jnp.concatenate([mine[0], mine[1]], axis=1)

    new_master, new_first, new_second = (own(v) for v in news)
    params = new_master.astype(jnp.bfloat16)
    return (
        new_master.T[None],
        new_first.T[None],
        new_second.T[None],
        params.T[None],
        checksum.reshape(1, -1),
    )


def solution(mesh):
    named = Mesh(mesh.devices.reshape(YL, C, YH, Z, X), REP + FSDP)
    state = P(REP, None, FSDP)
    placed = (P(REP, FSDP, None, None), state, state, state, P(FSDP), P(), P(), P())
    return jax.shard_map(
        shards,
        mesh=named,
        in_specs=placed,
        out_specs=(state, state, state, state, P(REP, None)),
        check_vma=False,
    )
```

```python
import jax
import jax.numpy as jnp
from jax import lax
from jax.experimental import pallas as pl
from jax.experimental.pallas import tpu as pltpu
from jax.sharding import Mesh, PartitionSpec as P

beta_one = 0.9
beta_two = 0.95
learn_rate = 0.05
decay_rate = 0.1
epsilon = 1e-08

YL, C, YH, ZQ, ZB, X = 4, 2, 2, 4, 2, 4
Z = ZQ * ZB
REP = ("yl", "c")
FSDP = ("yh", "zq", "zb", "x")
WIDTH, HALF, FEAT = 96, 64, 128


def swapped(value, axis, size, bit):
    return lax.ppermute(value, axis, [(i, i ^ bit) for i in range(size)])


def corrections(step_count):
    steps_done = step_count[0].astype(jnp.float32)
    correct_one = 1.0 - jnp.power(jnp.float32(beta_one), steps_done)
    correct_two = 1.0 - jnp.power(jnp.float32(beta_two), steps_done)
    return correct_one, correct_two


def adamw_update(master, first, second, grad, correct_one, correct_two):
    new_first = beta_one * first + (1.0 - beta_one) * grad
    new_second = beta_two * second + (1.0 - beta_two) * (grad * grad)
    update = new_first / correct_one / (jnp.sqrt(new_second / correct_two) + epsilon)
    new_master = master - learn_rate * (update + decay_rate * master)
    return (new_master, new_first, new_second)


def give_kernel(half_ref, grad_ref, master_ref, first_ref, second_ref, turned_ref):
    turn_kernel(half_ref, grad_ref, turned_ref)
    start = Z * X * WIDTH
    for i, state_ref in enumerate((master_ref, first_ref, second_ref)):
        turned_ref[start + i * WIDTH : start + (i + 1) * WIDTH, :] = state_ref[...]


def turn_kernel(half_ref, grad_ref, turned_ref):
    columns = Z * X * WIDTH
    for z in range(Z):
        first = grad_ref[:, z * X * WIDTH : (z + 1) * X * WIDTH]
        second = grad_ref[:, columns + z * X * WIDTH : columns + (z + 1) * X * WIDTH]
        value = jnp.concatenate([first, second], axis=0).T.astype(jnp.float32)
        for x in range(X):
            place = ((z % ZB * X + x) * ZQ + z // ZB) * WIDTH
            turned_ref[place : place + WIDTH, :] = value[x * WIDTH : (x + 1) * WIDTH]


def turned(grad, half, *state):
    columns = Z * X * WIDTH
    rows = columns + len(state) * WIDTH
    return pl.pallas_call(
        give_kernel if state else turn_kernel,
        grid_spec=pltpu.PrefetchScalarGridSpec(
            num_scalar_prefetch=1,
            grid=(1,),
            in_specs=[pl.BlockSpec((HALF, YH * columns), lambda i, half_ref: (half_ref[0], 0))]
            + [pl.BlockSpec((WIDTH, FEAT), lambda i, half_ref: (0, 0))] * len(state),
            out_specs=pl.BlockSpec(memory_space=pltpu.VMEM),
        ),
        out_shape=pltpu.VMEM((rows, FEAT), jnp.float32),
        cost_estimate=pl.CostEstimate(flops=0, bytes_accessed=columns * FEAT * 6, transcendentals=0),
    )(half.reshape(1), grad, *state)


def chip_sum(grad_parts, state, *beside):
    core = lax.axis_index("c")
    grad = grad_parts[0, 0]
    given = swapped(turned(grad, 1 - core, *state), "c", C, 1)
    columns = Z * X * WIDTH
    kept, *beside = lax.optimization_barrier((turned(grad, core), *beside))
    return kept + given[:columns], given[columns:], *beside


def near_grad(chip):
    blocks = lax.all_to_all(
        chip.reshape(ZB * X, ZQ * WIDTH, FEAT), ("zb", "x"), 0, 0, tiled=True
    )
    return jnp.sum(blocks, axis=0).reshape(ZQ, WIDTH, FEAT)


def reduced_grad(near, beside):
    plane = jnp.sum(lax.all_to_all(near, "zq", 0, 0, tiled=True), axis=0)
    plane, beside = lax.optimization_barrier((plane, beside))
    spread = jnp.broadcast_to(plane, (YH * YL, WIDTH, FEAT))
    lines = lax.all_to_all(spread, ("yh", "yl"), 0, 0, tiled=True)
    line = jnp.sum(lines, axis=0)
    return lax.all_gather(line, "c", axis=0, tiled=False), beside


def way_to_donor(flagged, source):
    match = flagged % (YH * Z * X) == lax.axis_index(FSDP)
    replica = flagged // (YH * Z * X)
    way = jnp.sum(jnp.where(match, replica ^ source, 0))
    return way, jnp.any(match & (replica == lax.axis_index(REP)))


def healed_state(state, other, way, flagged_here):
    moved = jnp.where((way & 1) != 0, other, state)
    for bit, place in ((1, 2), (2, 4)):
        other = swapped(moved, "yl", YL, bit)
        moved = jnp.where((way & place) != 0, other, moved)
    return jnp.where(flagged_here, moved, state)


def shards(grad_parts, master, moment1, moment2, probe, flagged, source, step_count):
    my_half = lax.axis_index("yh")
    state = (master[0].T, moment1[0].T, moment2[0].T)
    chip, other, way, flagged_here, correct = chip_sum(
        grad_parts, state, *way_to_donor(flagged, source), corrections(step_count)
    )
    state = jnp.concatenate(state)
    healed = healed_state(state, other, way, flagged_here)
    near, healed = lax.optimization_barrier((near_grad(chip), healed))
    weights = jnp.pad(jnp.broadcast_to(probe, (8, WIDTH)), ((0, 0), (0, FEAT - WIDTH)))
    mine = jnp.concatenate([healed, weights])
    other = swapped(mine, "yh", YH, 1)
    low, high = jnp.where(my_half == 0, mine, other), jnp.where(my_half == 0, other, mine)
    packed = jnp.stack(
        [
            jnp.concatenate([low[: 3 * WIDTH, :HALF], high[: 3 * WIDTH, :HALF]], axis=1),
            jnp.concatenate([low[: 3 * WIDTH, HALF:], high[: 3 * WIDTH, HALF:]], axis=1),
        ]
    )
    first_lanes = lax.broadcasted_iota(jnp.int32, (WIDTH, FEAT), 1) < HALF
    weights = jnp.where(
        first_lanes, low[3 * WIDTH, :WIDTH, None], high[3 * WIDTH, :WIDTH, None]
    )
    grad, (packed, weights) = reduced_grad(near, (packed, weights))
    states = packed.reshape(C, 3, WIDTH, FEAT)
    news = adamw_update(states[:, 0], states[:, 1], states[:, 2], grad, *correct)
    lane_sums = jnp.sum(news[0] * weights, axis=1)
    local_sums = (lane_sums[:, :HALF] + lane_sums[:, HALF:]).reshape(FEAT)
    spread = jnp.broadcast_to(local_sums, (Z * X, FEAT))
    checksum = jnp.sum(lax.all_to_all(spread, ("zq", "zb", "x"), 0, 0, tiled=True), axis=0)

    def own(value):
        mine = jnp.where(my_half == 0, value[:, :, :HALF], value[:, :, HALF:])
        return jnp.concatenate([mine[0], mine[1]], axis=1)

    new_master, new_first, new_second = (own(v) for v in news)
    params = new_master.astype(jnp.bfloat16)
    return (
        new_master.T[None],
        new_first.T[None],
        new_second.T[None],
        params.T[None],
        checksum.reshape(1, -1),
    )


def solution(mesh):
    named = Mesh(mesh.devices.reshape(YL, C, YH, ZQ, ZB, X), REP + FSDP)
    state = P(REP, None, FSDP)
    placed = (P(REP, FSDP, None, None), state, state, state, P(FSDP), P(), P(), P())
    return jax.shard_map(
        shards,
        mesh=named,
        in_specs=placed,
        out_specs=(state, state, state, state, P(REP, None)),
        check_vma=False,
    )
```

```python
import itertools

import jax
import jax.numpy as jnp
from jax import lax
from jax.experimental import pallas as pl
from jax.experimental.pallas import tpu as pltpu
from jax.sharding import Mesh, PartitionSpec as P

beta_one = 0.9
beta_two = 0.95
learn_rate = 0.05
decay_rate = 0.1
epsilon = 1e-08

YL, C, YH, Z, X = 4, 2, 2, 8, 4
REP = ("yl", "c")
FSDP = ("yh", "z", "x")
WIDTH, HALF, FEAT, ROWS = 96, 64, 128, 48


def swapped(value, axis, size, bit):
    return lax.ppermute(value, axis, [(i, i ^ bit) for i in range(size)])


def corrections(step_count):
    steps_done = step_count[0].astype(jnp.float32)
    correct_one = 1.0 - jnp.power(jnp.float32(beta_one), steps_done)
    correct_two = 1.0 - jnp.power(jnp.float32(beta_two), steps_done)
    return correct_one, correct_two


def adamw_update(master, first, second, grad, correct_one, correct_two):
    new_first = beta_one * first + (1.0 - beta_one) * grad
    new_second = beta_two * second + (1.0 - beta_two) * (grad * grad)
    update = new_first / correct_one / (jnp.sqrt(new_second / correct_two) + epsilon)
    new_master = master - learn_rate * (update + decay_rate * master)
    return (new_master, new_first, new_second)


def give_kernel(half_ref, grad_ref, master_ref, first_ref, second_ref, turned_ref):
    turn_kernel(half_ref, grad_ref, turned_ref)
    start = Z * X * WIDTH
    for i, state_ref in enumerate((master_ref, first_ref, second_ref)):
        turned_ref[start + i * WIDTH : start + (i + 1) * WIDTH, :] = state_ref[...]


def near_place(core, z, x):
    z, x = (z - core) % Z, (x - core) % X
    return z % 2 * 2 + x % 2, z // 2 * 2 + x // 2


def turn_kernel(half_ref, grad_ref, turned_ref):
    columns = Z * X * WIDTH
    wide = X * WIDTH
    for half in range(C):

        @pl.when(half_ref[0] == half)
        def _():
            for z in range(Z):
                first = grad_ref[:, z * wide : (z + 1) * wide]
                second = grad_ref[:, columns + z * wide : columns + (z + 1) * wide]
                value = jnp.concatenate([first, second], axis=0).T.astype(jnp.float32)
                for x in range(X):
                    near, far = near_place(half, z, x)
                    row = (near * 8 + far) * WIDTH
                    turned_ref[row : row + WIDTH, :] = value[x * WIDTH : (x + 1) * WIDTH]


def turned(grad, half, *state):
    columns = Z * X * WIDTH
    rows = columns + len(state) * WIDTH
    return pl.pallas_call(
        give_kernel if state else turn_kernel,
        grid_spec=pltpu.PrefetchScalarGridSpec(
            num_scalar_prefetch=1,
            grid=(1,),
            in_specs=[pl.BlockSpec((HALF, YH * columns), lambda i, half_ref: (half_ref[0], 0))]
            + [pl.BlockSpec((WIDTH, FEAT), lambda i, half_ref: (0, 0))] * len(state),
            out_specs=pl.BlockSpec(memory_space=pltpu.VMEM),
        ),
        out_shape=pltpu.VMEM((rows, FEAT), jnp.float32),
        cost_estimate=pl.CostEstimate(flops=0, bytes_accessed=columns * FEAT * 6, transcendentals=0),
    )(half.reshape(1), grad, *state)


def chip_sum(grad_parts, state, *beside):
    core = lax.axis_index("c")
    grad = grad_parts[0, 0]
    given = swapped(turned(grad, 1 - core, *state), "c", C, 1)
    columns = Z * X * WIDTH
    kept, *beside = lax.optimization_barrier((turned(grad, core), *beside))
    return kept + given[:columns], given[columns:], *beside


def groups(over_near):
    found = {}
    for yl, c, yh, z, x in itertools.product(*map(range, (YL, C, YH, Z, X))):
        near, far = near_place(c, z, x)
        rank, rest = (near, far) if over_near else (far, near)
        device = (((yl * C + c) * YH + yh) * Z + z) * X + x
        found.setdefault((yl, c, yh, rest), {})[rank] = device
    return [[members[rank] for rank in sorted(members)] for members in found.values()]


def exchanged(blocks, over_near):
    every = ("yl", "c", "yh", "z", "x")
    return lax.all_to_all(blocks, every, 0, 0, tiled=True, axis_index_groups=groups(over_near))


def two_up(value, lanes):
    part = value[..., lanes * HALF : (lanes + 1) * HALF]
    return jnp.concatenate([part[..., :ROWS, :], part[..., ROWS:, :]], axis=-1)


def line_grad(plane):
    spread = jnp.stack([two_up(plane, half) for half in range(YH) for _ in range(YL)])
    lines = lax.all_to_all(spread, ("yh", "yl"), 0, 0, tiled=True)
    return lax.all_gather(jnp.sum(lines, axis=0), "c", axis=0, tiled=False)


def stage(moved, way, axis, size, bit, place):
    return jnp.where((way & place) != 0, swapped(moved, axis, size, bit), moved)


def way_to_donor(flagged, source):
    match = flagged % (YH * Z * X) == lax.axis_index(FSDP)
    replica = flagged // (YH * Z * X)
    way = jnp.sum(jnp.where(match, replica ^ source, 0))
    return way, jnp.any(match & (replica == lax.axis_index(REP)))


def shards(grad_parts, master, moment1, moment2, probe, flagged, source, step_count):
    state = (master[0].T, moment1[0].T, moment2[0].T)
    chip, other, way, flagged_here, correct = chip_sum(
        grad_parts, state, *way_to_donor(flagged, source), corrections(step_count)
    )
    state = jnp.concatenate(state)
    moved = jnp.where((way & 1) != 0, other, state)
    blocks = exchanged(chip.reshape(4, 8 * WIDTH, FEAT), True)
    near = jnp.sum(blocks, axis=0).reshape(8, WIDTH, FEAT)
    near, moved = lax.optimization_barrier((near, stage(moved, way, "yl", YL, 2, 4)))
    plane = jnp.sum(exchanged(near, False), axis=0)
    plane, moved = lax.optimization_barrier((plane, stage(moved, way, "yl", YL, 1, 2)))
    healed = jnp.where(flagged_here, moved, state).reshape(3, WIDTH, FEAT)
    packed = jnp.stack([two_up(healed, half) for half in range(C)])
    upper = lax.broadcasted_iota(jnp.int32, (ROWS, FEAT), 1) < HALF
    weights = jnp.where(upper, probe[:ROWS, None], probe[ROWS:, None])
    plane, packed, weights = lax.optimization_barrier((plane, packed, weights))
    grad = line_grad(plane)
    news = adamw_update(packed[:, 0], packed[:, 1], packed[:, 2], grad, *correct)
    lane_sums = jnp.sum(news[0] * weights, axis=1)
    local_sums = (lane_sums[:, :HALF] + lane_sums[:, HALF:]).reshape(FEAT)
    spread = jnp.broadcast_to(local_sums, (YH * Z * X, FEAT))
    checksum = jnp.sum(lax.all_to_all(spread, FSDP, 0, 0, tiled=True), axis=0)

    def own(value):
        upper = jnp.concatenate([value[0, :, :HALF], value[1, :, :HALF]], axis=1)
        lower = jnp.concatenate([value[0, :, HALF:], value[1, :, HALF:]], axis=1)
        return jnp.concatenate([upper, lower])

    new_master, new_first, new_second = (own(v) for v in news)
    params = new_master.astype(jnp.bfloat16)
    return (
        new_master.T[None],
        new_first.T[None],
        new_second.T[None],
        params.T[None],
        checksum.reshape(1, -1),
    )


def solution(mesh):
    named = Mesh(mesh.devices.reshape(YL, C, YH, Z, X), REP + FSDP)
    state = P(REP, None, FSDP)
    placed = (P(REP, FSDP, None, None), state, state, state, P(FSDP), P(), P(), P())
    return jax.shard_map(
        shards,
        mesh=named,
        in_specs=placed,
        out_specs=(state, state, state, state, P(REP, None)),
        check_vma=False,
    )
```

```python
import itertools

import jax
import jax.numpy as jnp
from jax import lax
from jax.experimental import pallas as pl
from jax.experimental.pallas import tpu as pltpu
from jax.sharding import Mesh, PartitionSpec as P

beta_one = 0.9
beta_two = 0.95
learn_rate = 0.05
decay_rate = 0.1
epsilon = 1e-08

YL, C, YH, Z, X = 4, 2, 2, 8, 4
REP = ("yl", "c")
FSDP = ("yh", "z", "x")
WIDTH, HALF, FEAT, ROWS = 96, 64, 128, 48


def swapped(value, axis, size, bit):
    return lax.ppermute(value, axis, [(i, i ^ bit) for i in range(size)])


def corrections(step_count):
    steps_done = step_count[0].astype(jnp.float32)
    correct_one = 1.0 - jnp.power(jnp.float32(beta_one), steps_done)
    correct_two = 1.0 - jnp.power(jnp.float32(beta_two), steps_done)
    return correct_one, correct_two


def adamw_update(master, first, second, grad, correct_one, correct_two):
    new_first = beta_one * first + (1.0 - beta_one) * grad
    new_second = beta_two * second + (1.0 - beta_two) * (grad * grad)
    update = new_first / correct_one / (jnp.sqrt(new_second / correct_two) + epsilon)
    new_master = master - learn_rate * (update + decay_rate * master)
    return (new_master, new_first, new_second)


def give_kernel(half_ref, grad_ref, master_ref, first_ref, second_ref, turned_ref):
    turn_kernel(half_ref, grad_ref, turned_ref)
    start = Z * X * WIDTH
    for i, state_ref in enumerate((master_ref, first_ref, second_ref)):
        turned_ref[start + i * WIDTH : start + (i + 1) * WIDTH, :] = state_ref[...]


def near_place(core, z, x):
    z, x = (z - core) % Z, (x - core) % X
    return z % 2 * 2 + x % 2, z // 2 * 2 + x // 2


def turn_kernel(half_ref, grad_ref, turned_ref):
    columns = Z * X * WIDTH
    wide = X * WIDTH
    for half in range(C):

        @pl.when(half_ref[0] == half)
        def _():
            for z in range(Z):
                first = grad_ref[:, z * wide : (z + 1) * wide]
                second = grad_ref[:, columns + z * wide : columns + (z + 1) * wide]
                value = jnp.concatenate([first, second], axis=0).T.astype(jnp.float32)
                for x in range(X):
                    near, far = near_place(half, z, x)
                    row = (near * 8 + far) * WIDTH
                    turned_ref[row : row + WIDTH, :] = value[x * WIDTH : (x + 1) * WIDTH]


def turned(grad, half, *state):
    columns = Z * X * WIDTH
    rows = columns + len(state) * WIDTH
    return pl.pallas_call(
        give_kernel if state else turn_kernel,
        grid_spec=pltpu.PrefetchScalarGridSpec(
            num_scalar_prefetch=1,
            grid=(1,),
            in_specs=[pl.BlockSpec((HALF, YH * columns), lambda i, half_ref: (half_ref[0], 0))]
            + [pl.BlockSpec((WIDTH, FEAT), lambda i, half_ref: (0, 0))] * len(state),
            out_specs=pl.BlockSpec(memory_space=pltpu.VMEM),
        ),
        out_shape=pltpu.VMEM((rows, FEAT), jnp.float32),
        cost_estimate=pl.CostEstimate(flops=0, bytes_accessed=columns * FEAT * 6, transcendentals=0),
    )(half.reshape(1), grad, *state)


def chip_sum(grad_parts, state, *beside):
    core = lax.axis_index("c")
    grad = grad_parts[0, 0]
    given = swapped(turned(grad, 1 - core, *state), "c", C, 1)
    columns = Z * X * WIDTH
    kept, *beside = lax.optimization_barrier((turned(grad, core), *beside))
    return kept + given[:columns], given[columns:], *beside


def groups(over_near):
    found = {}
    for yl, c, yh, z, x in itertools.product(*map(range, (YL, C, YH, Z, X))):
        near, far = near_place(c, z, x)
        rank, rest = (near, far) if over_near else (far, near)
        device = (((yl * C + c) * YH + yh) * Z + z) * X + x
        found.setdefault((yl, c, yh, rest), {})[rank] = device
    return [[members[rank] for rank in sorted(members)] for members in found.values()]


def exchanged(blocks, over_near):
    every = ("yl", "c", "yh", "z", "x")
    return lax.all_to_all(blocks, every, 0, 0, tiled=True, axis_index_groups=groups(over_near))


def two_up(value, lanes):
    part = value[..., lanes * HALF : (lanes + 1) * HALF]
    return jnp.concatenate([part[..., :ROWS, :], part[..., ROWS:, :]], axis=-1)


def line_grad(plane):
    spread = jnp.stack([two_up(plane, half) for half in range(YH) for _ in range(YL)])
    lines = lax.all_to_all(spread, ("yh", "yl"), 0, 0, tiled=True)
    return lax.all_gather(jnp.sum(lines, axis=0), "c", axis=0, tiled=False)


def stage(moved, way, axis, size, bit, place):
    return jnp.where((way & place) != 0, swapped(moved, axis, size, bit), moved)


def way_to_donor(flagged, source):
    match = flagged % (YH * Z * X) == lax.axis_index(FSDP)
    replica = flagged // (YH * Z * X)
    way = jnp.sum(jnp.where(match, replica ^ source, 0))
    return way, jnp.any(match & (replica == lax.axis_index(REP)))


def shards(grad_parts, master, moment1, moment2, probe, flagged, source, step_count):
    state = (master[0].T, moment1[0].T, moment2[0].T)
    chip, other, way, flagged_here, correct = chip_sum(
        grad_parts, state, *way_to_donor(flagged, source), corrections(step_count)
    )
    state = jnp.concatenate(state)
    moved = jnp.where((way & 1) != 0, other, state)
    blocks = exchanged(chip.reshape(4, 8 * WIDTH, FEAT), True)
    near = jnp.sum(blocks, axis=0).reshape(8, WIDTH, FEAT)
    near, moved = lax.optimization_barrier((near, stage(moved, way, "yl", YL, 2, 4)))
    plane = jnp.sum(exchanged(near, False), axis=0)
    moved = stage(moved, way, "yl", YL, 1, 2)
    plane, healed = lax.optimization_barrier((plane, jnp.where(flagged_here, moved, state)))
    healed = healed.reshape(3, WIDTH, FEAT)
    packed = jnp.stack([two_up(healed, half) for half in range(C)])
    upper = lax.broadcasted_iota(jnp.int32, (ROWS, FEAT), 1) < HALF
    weights = jnp.where(upper, probe[:ROWS, None], probe[ROWS:, None])
    plane, packed, weights = lax.optimization_barrier((plane, packed, weights))
    grad = line_grad(plane)
    news = adamw_update(packed[:, 0], packed[:, 1], packed[:, 2], grad, *correct)
    lane_sums = jnp.sum(news[0] * weights, axis=1)
    local_sums = (lane_sums[:, :HALF] + lane_sums[:, HALF:]).reshape(FEAT)
    spread = jnp.broadcast_to(local_sums, (YH * Z * X, FEAT))
    checksum = jnp.sum(lax.all_to_all(spread, FSDP, 0, 0, tiled=True), axis=0)

    def own(value):
        upper = jnp.concatenate([value[0, :, :HALF], value[1, :, :HALF]], axis=1)
        lower = jnp.concatenate([value[0, :, HALF:], value[1, :, HALF:]], axis=1)
        return jnp.concatenate([upper, lower])

    new_master, new_first, new_second = (own(v) for v in news)
    params = new_master.astype(jnp.bfloat16)
    return (
        new_master.T[None],
        new_first.T[None],
        new_second.T[None],
        params.T[None],
        checksum.reshape(1, -1),
    )


def solution(mesh):
    named = Mesh(mesh.devices.reshape(YL, C, YH, Z, X), REP + FSDP)
    state = P(REP, None, FSDP)
    placed = (P(REP, FSDP, None, None), state, state, state, P(FSDP), P(), P(), P())
    return jax.shard_map(
        shards,
        mesh=named,
        in_specs=placed,
        out_specs=(state, state, state, state, P(REP, None)),
        check_vma=False,
    )
```

```python
import itertools

import jax
import jax.numpy as jnp
from jax import lax
from jax.experimental import pallas as pl
from jax.experimental.pallas import tpu as pltpu
from jax.sharding import Mesh, PartitionSpec as P

beta_one = 0.9
beta_two = 0.95
learn_rate = 0.05
decay_rate = 0.1
epsilon = 1e-08

YL, C, YH, Z, X = 4, 2, 2, 8, 4
REP = ("yl", "c")
FSDP = ("yh", "z", "x")
WIDTH, HALF, FEAT, ROWS = 96, 64, 128, 48


def swapped(value, axis, size, bit):
    return lax.ppermute(value, axis, [(i, i ^ bit) for i in range(size)])


def corrections(step_count):
    steps_done = step_count[0].astype(jnp.float32)
    correct_one = 1.0 - jnp.power(jnp.float32(beta_one), steps_done)
    correct_two = 1.0 - jnp.power(jnp.float32(beta_two), steps_done)
    return correct_one, correct_two


def adamw_update(master, first, second, grad, correct_one, correct_two):
    new_first = beta_one * first + (1.0 - beta_one) * grad
    new_second = beta_two * second + (1.0 - beta_two) * (grad * grad)
    update = new_first / correct_one / (jnp.sqrt(new_second / correct_two) + epsilon)
    new_master = master - learn_rate * (update + decay_rate * master)
    return (new_master, new_first, new_second)


def near_place(core, z, x):
    z, x = (z - core) % Z, (x - core) % X
    return z % 2 * 2 + x % 2, z // 2 * 2 + x // 2


def turn_columns(half, zs, grad_ref, turned_ref):
    columns = Z * X * WIDTH
    wide = X * WIDTH
    for z in zs:
        first = grad_ref[:, z * wide : (z + 1) * wide]
        second = grad_ref[:, columns + z * wide : columns + (z + 1) * wide]
        value = jnp.concatenate([first, second], axis=0).T.astype(jnp.float32)
        for x in range(X):
            near, far = near_place(half, z, x)
            row = (near * 8 + far) * WIDTH
            turned_ref[row : row + WIDTH, :] = value[x * WIDTH : (x + 1) * WIDTH]


def turn_kernel(half_ref, grad_ref, turned_ref):
    for half in range(C):

        @pl.when(half_ref[0] == half)
        def _():
            turn_columns(half, range(Z), grad_ref, turned_ref)


def give_kernel(half_ref, grad_ref, master_ref, first_ref, second_ref, out_ref, turned_ref, sems):
    columns = Z * X * WIDTH
    states = [
        pltpu.make_async_copy(
            ref, out_ref.at[pl.ds(columns + i * WIDTH, WIDTH)], sems.at[2 + i]
        )
        for i, ref in enumerate((master_ref, first_ref, second_ref))
    ]
    for copy in states:
        copy.start()
    for half in range(C):

        @pl.when(half_ref[0] == half)
        def _():
            parts = []
            for part in range(2):
                zs = [(2 * i + part + half) % Z for i in range(Z // 2)]
                turn_columns(half, zs, grad_ref, turned_ref)
                rows = pl.ds(part * columns // 2, columns // 2)
                parts.append(
                    pltpu.make_async_copy(turned_ref.at[rows], out_ref.at[rows], sems.at[part])
                )
                parts[part].start()
            for copy in parts:
                copy.wait()

    for copy in states:
        copy.wait()


def turned(grad, half, *state):
    columns = Z * X * WIDTH
    rows = columns + len(state) * WIDTH
    return pl.pallas_call(
        give_kernel if state else turn_kernel,
        grid_spec=pltpu.PrefetchScalarGridSpec(
            num_scalar_prefetch=1,
            grid=(1,),
            in_specs=[pl.BlockSpec((HALF, YH * columns), lambda i, half_ref: (half_ref[0], 0))]
            + [pl.BlockSpec((WIDTH, FEAT), lambda i, half_ref: (0, 0))] * len(state),
            out_specs=pl.BlockSpec(memory_space=pl.ANY if state else pltpu.VMEM),
            scratch_shapes=[pltpu.VMEM((columns, FEAT), jnp.float32), pltpu.SemaphoreType.DMA((5,))]
            if state
            else [],
        ),
        out_shape=(jax.ShapeDtypeStruct if state else pltpu.VMEM)((rows, FEAT), jnp.float32),
        cost_estimate=pl.CostEstimate(flops=0, bytes_accessed=columns * FEAT * 6, transcendentals=0),
    )(half.reshape(1), grad, *state)


def chip_sum(grad_parts, state, *beside):
    core = lax.axis_index("c")
    grad = grad_parts[0, 0]
    given = swapped(turned(grad, 1 - core, *state), "c", C, 1)
    columns = Z * X * WIDTH
    kept, *beside = lax.optimization_barrier((turned(grad, core), *beside))
    return kept + given[:columns], given[columns:], *beside


def groups(over_near):
    found = {}
    for yl, c, yh, z, x in itertools.product(*map(range, (YL, C, YH, Z, X))):
        near, far = near_place(c, z, x)
        rank, rest = (near, far) if over_near else (far, near)
        device = (((yl * C + c) * YH + yh) * Z + z) * X + x
        found.setdefault((yl, c, yh, rest), {})[rank] = device
    return [[members[rank] for rank in sorted(members)] for members in found.values()]


def exchanged(blocks, over_near):
    every = ("yl", "c", "yh", "z", "x")
    return lax.all_to_all(blocks, every, 0, 0, tiled=True, axis_index_groups=groups(over_near))


def two_up(value, lanes):
    part = value[..., lanes * HALF : (lanes + 1) * HALF]
    return jnp.concatenate([part[..., :ROWS, :], part[..., ROWS:, :]], axis=-1)


def line_grad(plane):
    spread = jnp.stack([two_up(plane, half) for half in range(YH) for _ in range(YL)])
    lines = lax.all_to_all(spread, ("yh", "yl"), 0, 0, tiled=True)
    return lax.all_gather(jnp.sum(lines, axis=0), "c", axis=0, tiled=False)


def stage(moved, way, axis, size, bit, place):
    return jnp.where((way & place) != 0, swapped(moved, axis, size, bit), moved)


def way_to_donor(flagged, source):
    match = flagged % (YH * Z * X) == lax.axis_index(FSDP)
    replica = flagged // (YH * Z * X)
    way = jnp.sum(jnp.where(match, replica ^ source, 0))
    return way, jnp.any(match & (replica == lax.axis_index(REP)))


def shards(grad_parts, master, moment1, moment2, probe, flagged, source, step_count):
    state = (master[0].T, moment1[0].T, moment2[0].T)
    chip, other, way, flagged_here, correct = chip_sum(
        grad_parts, state, *way_to_donor(flagged, source), corrections(step_count)
    )
    state = jnp.concatenate(state)
    moved = jnp.where((way & 1) != 0, other, state)
    blocks = exchanged(chip.reshape(4, 8 * WIDTH, FEAT), True)
    near = jnp.sum(blocks, axis=0).reshape(8, WIDTH, FEAT)
    near, moved = lax.optimization_barrier((near, stage(moved, way, "yl", YL, 2, 4)))
    plane = jnp.sum(exchanged(near, False), axis=0)
    moved = stage(moved, way, "yl", YL, 1, 2)
    plane, healed = lax.optimization_barrier((plane, jnp.where(flagged_here, moved, state)))
    healed = healed.reshape(3, WIDTH, FEAT)
    packed = jnp.stack([two_up(healed, half) for half in range(C)])
    upper = lax.broadcasted_iota(jnp.int32, (ROWS, FEAT), 1) < HALF
    weights = jnp.where(upper, probe[:ROWS, None], probe[ROWS:, None])
    plane, packed, weights = lax.optimization_barrier((plane, packed, weights))
    grad = line_grad(plane)
    news = adamw_update(packed[:, 0], packed[:, 1], packed[:, 2], grad, *correct)
    lane_sums = jnp.sum(news[0] * weights, axis=1)
    local_sums = (lane_sums[:, :HALF] + lane_sums[:, HALF:]).reshape(FEAT)
    spread = jnp.broadcast_to(local_sums, (YH * Z * X, FEAT))
    checksum = jnp.sum(lax.all_to_all(spread, FSDP, 0, 0, tiled=True), axis=0)

    def own(value):
        upper = jnp.concatenate([value[0, :, :HALF], value[1, :, :HALF]], axis=1)
        lower = jnp.concatenate([value[0, :, HALF:], value[1, :, HALF:]], axis=1)
        return jnp.concatenate([upper, lower])

    new_master, new_first, new_second = (own(v) for v in news)
    params = new_master.astype(jnp.bfloat16)
    return (
        new_master.T[None],
        new_first.T[None],
        new_second.T[None],
        params.T[None],
        checksum.reshape(1, -1),
    )


def solution(mesh):
    named = Mesh(mesh.devices.reshape(YL, C, YH, Z, X), REP + FSDP)
    state = P(REP, None, FSDP)
    placed = (P(REP, FSDP, None, None), state, state, state, P(FSDP), P(), P(), P())
    return jax.shard_map(
        shards,
        mesh=named,
        in_specs=placed,
        out_specs=(state, state, state, state, P(REP, None)),
        check_vma=False,
    )
```

```python
import itertools

import jax
import jax.numpy as jnp
from jax import lax
from jax.experimental import pallas as pl
from jax.experimental.pallas import tpu as pltpu
from jax.sharding import Mesh, PartitionSpec as P

beta_one = 0.9
beta_two = 0.95
learn_rate = 0.05
decay_rate = 0.1
epsilon = 1e-08

YL, C, YH, Z, X = 4, 2, 2, 8, 4
REP = ("yl", "c")
FSDP = ("yh", "z", "x")
WIDTH, HALF, FEAT, ROWS = 96, 64, 128, 48


def swapped(value, axis, size, bit):
    return lax.ppermute(value, axis, [(i, i ^ bit) for i in range(size)])


def corrections(step_count):
    steps_done = step_count[0].astype(jnp.float32)
    correct_one = 1.0 - jnp.power(jnp.float32(beta_one), steps_done)
    correct_two = 1.0 - jnp.power(jnp.float32(beta_two), steps_done)
    return correct_one, correct_two


def adamw_update(master, first, second, grad, correct_one, correct_two):
    new_first = beta_one * first + (1.0 - beta_one) * grad
    new_second = beta_two * second + (1.0 - beta_two) * (grad * grad)
    update = new_first / correct_one / (jnp.sqrt(new_second / correct_two) + epsilon)
    new_master = master - learn_rate * (update + decay_rate * master)
    return (new_master, new_first, new_second)


def near_place(core, z, x):
    z, x = (z - core) % Z, (x - core) % X
    return z % 2 * 2 + x % 2, z // 2 * 2 + x // 2


def turn_columns(half, zs, grad_ref, turned_ref):
    columns = Z * X * WIDTH
    wide = X * WIDTH
    for z in zs:
        first = grad_ref[:, z * wide : (z + 1) * wide]
        second = grad_ref[:, columns + z * wide : columns + (z + 1) * wide]
        value = jnp.concatenate([first, second], axis=0).T.astype(jnp.float32)
        for x in range(X):
            near, far = near_place(half, z, x)
            row = (near * 8 + far) * WIDTH
            turned_ref[row : row + WIDTH, :] = value[x * WIDTH : (x + 1) * WIDTH]


def turn_kernel(half_ref, grad_ref, turned_ref):
    for half in range(C):

        @pl.when(half_ref[0] == half)
        def _():
            turn_columns(half, range(Z), grad_ref, turned_ref)


def give_kernel(half_ref, grad_ref, master_ref, first_ref, second_ref, out_ref, turned_ref, sems):
    columns = Z * X * WIDTH
    states = [
        pltpu.make_async_copy(
            ref, out_ref.at[pl.ds(columns + i * WIDTH, WIDTH)], sems.at[2 + i]
        )
        for i, ref in enumerate((master_ref, first_ref, second_ref))
    ]
    for copy in states:
        copy.start()
    for half in range(C):

        @pl.when(half_ref[0] == half)
        def _():
            parts = []
            for part in range(2):
                zs = [(2 * i + part + half) % Z for i in range(Z // 2)]
                turn_columns(half, zs, grad_ref, turned_ref)
                rows = pl.ds(part * columns // 2, columns // 2)
                parts.append(
                    pltpu.make_async_copy(turned_ref.at[rows], out_ref.at[rows], sems.at[part])
                )
                parts[part].start()
            for copy in parts:
                copy.wait()

    for copy in states:
        copy.wait()


def turned(grad, half, *state):
    columns = Z * X * WIDTH
    rows = columns + len(state) * WIDTH
    return pl.pallas_call(
        give_kernel if state else turn_kernel,
        grid_spec=pltpu.PrefetchScalarGridSpec(
            num_scalar_prefetch=1,
            grid=(1,),
            in_specs=[pl.BlockSpec((HALF, YH * columns), lambda i, half_ref: (half_ref[0], 0))]
            + [pl.BlockSpec((WIDTH, FEAT), lambda i, half_ref: (0, 0))] * len(state),
            out_specs=pl.BlockSpec(memory_space=pl.ANY if state else pltpu.VMEM),
            scratch_shapes=[pltpu.VMEM((columns, FEAT), jnp.float32), pltpu.SemaphoreType.DMA((5,))]
            if state
            else [],
        ),
        out_shape=(jax.ShapeDtypeStruct if state else pltpu.VMEM)((rows, FEAT), jnp.float32),
        cost_estimate=pl.CostEstimate(flops=0, bytes_accessed=columns * FEAT * 6, transcendentals=0),
    )(half.reshape(1), grad, *state)


def chip_sum(grad_parts, state, *beside):
    core = lax.axis_index("c")
    grad = grad_parts[0, 0]
    given = swapped(turned(grad, 1 - core, *state), "c", C, 1)
    columns = Z * X * WIDTH
    kept, *beside = lax.optimization_barrier((turned(grad, core), *beside))
    return kept + given[:columns], given[columns:], *beside


def groups(over_near):
    found = {}
    for yl, c, yh, z, x in itertools.product(*map(range, (YL, C, YH, Z, X))):
        near, far = near_place(c, z, x)
        rank, rest = (near, far) if over_near else (far, near)
        device = (((yl * C + c) * YH + yh) * Z + z) * X + x
        found.setdefault((yl, c, yh, rest), {})[rank] = device
    return [[members[rank] for rank in sorted(members)] for members in found.values()]


def exchanged(blocks, over_near):
    every = ("yl", "c", "yh", "z", "x")
    return lax.all_to_all(blocks, every, 0, 0, tiled=True, axis_index_groups=groups(over_near))


def two_up(value, lanes):
    part = value[..., lanes * HALF : (lanes + 1) * HALF]
    return jnp.concatenate([part[..., :ROWS, :], part[..., ROWS:, :]], axis=-1)


def line_grad(plane):
    spread = jnp.stack([two_up(plane, half) for half in range(YH) for _ in range(YL)])
    lines = lax.all_to_all(spread, ("yh", "yl"), 0, 0, tiled=True)
    return lax.all_gather(jnp.sum(lines, axis=0), "c", axis=0, tiled=False)


def stage(moved, way, axis, size, bit, place):
    return jnp.where((way & place) != 0, swapped(moved, axis, size, bit), moved)


def way_to_donor(flagged, source):
    match = flagged % (YH * Z * X) == lax.axis_index(FSDP)
    replica = flagged // (YH * Z * X)
    way = jnp.sum(jnp.where(match, replica ^ source, 0))
    return way, jnp.any(match & (replica == lax.axis_index(REP)))


def shards(grad_parts, master, moment1, moment2, probe, flagged, source, step_count):
    state = (master[0].T, moment1[0].T, moment2[0].T)
    chip, other, way, flagged_here, correct = chip_sum(
        grad_parts, state, *way_to_donor(flagged, source), corrections(step_count)
    )
    state = jnp.concatenate(state)
    moved = jnp.where((way & 1) != 0, other, state)
    blocks = exchanged(chip.reshape(4, 8 * WIDTH, FEAT), True)
    near = jnp.sum(blocks, axis=0).reshape(8, WIDTH, FEAT)
    cut = 3 * WIDTH // 2
    first = stage(moved[:cut], way, "yl", YL, 2, 4)
    second = stage(moved[cut:], way, "yl", YL, 1, 2)
    near, first, second = lax.optimization_barrier((near, first, second))
    plane = jnp.sum(exchanged(near, False), axis=0)
    first = jnp.where(flagged_here, stage(first, way, "yl", YL, 1, 2), state[:cut])
    second = jnp.where(flagged_here, stage(second, way, "yl", YL, 2, 4), state[cut:])
    plane, first, second = lax.optimization_barrier((plane, first, second))
    healed = jnp.concatenate([first, second]).reshape(3, WIDTH, FEAT)
    packed = jnp.stack([two_up(healed, half) for half in range(C)])
    upper = lax.broadcasted_iota(jnp.int32, (ROWS, FEAT), 1) < HALF
    weights = jnp.where(upper, probe[:ROWS, None], probe[ROWS:, None])
    plane, packed, weights = lax.optimization_barrier((plane, packed, weights))
    grad = line_grad(plane)
    news = adamw_update(packed[:, 0], packed[:, 1], packed[:, 2], grad, *correct)
    lane_sums = jnp.sum(news[0] * weights, axis=1)
    local_sums = (lane_sums[:, :HALF] + lane_sums[:, HALF:]).reshape(FEAT)
    spread = jnp.broadcast_to(local_sums, (YH * Z * X, FEAT))
    checksum = jnp.sum(lax.all_to_all(spread, FSDP, 0, 0, tiled=True), axis=0)

    def own(value):
        upper = jnp.concatenate([value[0, :, :HALF], value[1, :, :HALF]], axis=1)
        lower = jnp.concatenate([value[0, :, HALF:], value[1, :, HALF:]], axis=1)
        return jnp.concatenate([upper, lower])

    new_master, new_first, new_second = (own(v) for v in news)
    params = new_master.astype(jnp.bfloat16)
    return (
        new_master.T[None],
        new_first.T[None],
        new_second.T[None],
        params.T[None],
        checksum.reshape(1, -1),
    )


def solution(mesh):
    named = Mesh(mesh.devices.reshape(YL, C, YH, Z, X), REP + FSDP)
    state = P(REP, None, FSDP)
    placed = (P(REP, FSDP, None, None), state, state, state, P(FSDP), P(), P(), P())
    return jax.shard_map(
        shards,
        mesh=named,
        in_specs=placed,
        out_specs=(state, state, state, state, P(REP, None)),
        check_vma=False,
    )
```
